256 devices in a mesh: rep: 32 (over z_hi, y, x), fsdp: 8 (over z_lo, core).
Axes of the slice: x: 4, y: 4, z: 8 (z_hi: 2, z_lo: 4; z = z_hi * 4 + z_lo), core: 2. Of those that a mesh axis runs over, the one named last changes fastest.
Arguments:
- hidden: bfloat16 [65536, 4608], P(('rep', 'fsdp')), may hold values from -12 to 12
- lengths: int32 [256, 8], P(('rep', 'fsdp')), may hold values from 1 to 64, 256 in all within a row
- ranks: int32 [256, 8], P(('rep', 'fsdp')), may hold values from 0 to 7, each once within a row
- gain: bfloat16 [4608], P('fsdp'), may hold values from 0.5 to 1.5
- head: bfloat16 [4608], P('fsdp'), may hold values from -1 to 1
- local_frag: bfloat16 [32, 512, 4608], P('rep', 'fsdp'), may hold values from -6 to 6
- global_prev: float32 [512, 4608], P('fsdp'), may hold values from -4 to 4
- momentum: float32 [512, 4608], P('fsdp'), may hold values from -3 to 3
Outputs:
- d_hidden: bfloat16 [65536, 4608], P(('rep', 'fsdp'))
- grad_gain: float32 [32, 4608], P('rep', 'fsdp')
- grad_head: float32 [32, 4608], P('rep', 'fsdp')
- new_global: float32 [512, 4608], P('fsdp')
- new_momentum: float32 [512, 4608], P('fsdp')
- merged: bfloat16 [32, 512, 4608], P('rep', 'fsdp')
The draws below stay inside these ranges and needn't reach their ends.
Inputs may be any that keep to these rules, and one draw needn't show every extreme that they name: The 8 lengths of each list sum to 256, and the longest passage of each list has exactly 64 tokens. `ranks`: each row is a permutation of 0 to 7.
All inputs are finite; a program needn't handle non-finite values.
Results may differ from the reference program's by a relative error of at most 0.001.
Values may be sent and summed in bfloat16 or wider, within the bound.
No kernel may reach another device: no remote copies, remote signals or barrier semaphores. Data moves between devices by JAX's collectives and lax.ppermute only.
A program may use at most 64 MiB of HBM per device.

```python
import math
import jax
import jax.numpy as jnp
import numpy as np
from jax import lax

D = 4608
CAND = 8
LIST_LEN = 256
MOST = 64
TOKENS = 65536
LISTS = 256
FROWS = 512
N_REP = 32


TOP_SCORE = 40.0


def shared_direction(key):
    return jnp.clip(jax.random.normal(key, (D,), jnp.float32), -4.0, 4.0)


def draw_hidden(key, part):
    direction = shared_direction(key)
    key = jax.random.fold_in(key, 11)
    k_noise, k_pick, k_sign, k_level, k_token = jax.random.split(key, 5)
    list_count = TOKENS // LIST_LEN
    noise = jnp.clip(jax.random.normal(k_noise, (TOKENS, D), jnp.float32), -6.0, 6.0)
    picked = (jax.random.uniform(k_pick, (list_count, 1), jnp.float32) < 0.3).astype(jnp.float32)
    signs = jnp.where(jax.random.uniform(k_sign, (list_count, 1), jnp.float32) < 0.5, -1.0, 1.0)
    level = jax.random.uniform(k_level, (list_count, 1), jnp.float32, 0.3, 1.0) * (TOP_SCORE / math.sqrt(MOST))
    per_token = jax.random.uniform(k_token, (list_count, LIST_LEN), jnp.float32, 0.5, 1.5)
    strength = (picked * signs * level * per_token).reshape(TOKENS, 1) / math.sqrt(D)
    values = noise + strength * direction[None, :]
    return jnp.clip(values, -12.0, 12.0).astype(jnp.bfloat16)


def draw_head(key, part):
    direction = shared_direction(key)
    key = jax.random.fold_in(key, 23)
    extra = jnp.clip(jax.random.normal(key, (D,), jnp.float32), -4.0, 4.0)
    return ((direction + 0.5 * extra) / math.sqrt(D)).astype(jnp.bfloat16)


def steps_of(own_key, shape, cuts, low, top_value):
    level, own = 1.0, jax.random.fold_in(own_key, 6)
    for axis_at, blocks in cuts:
        steps = jnp.exp(jax.random.uniform(jax.random.fold_in(own, axis_at), (blocks,), jnp.float32, low / len(cuts), top_value / len(cuts)))
        level = level * jnp.repeat(steps, shape[axis_at] // blocks).reshape([-1 if axis == axis_at else 1 for axis in range(len(shape))])
    return level


def length_profile(number_of, total, limit, skew):
    weights = [(1 << 20) // math.isqrt(standing ** skew) + 1 for standing in range(2, number_of + 1)]
    rest, counts = total - limit - (number_of - 1), [1] * (number_of - 1)
    while rest > 0:
        movable = [i for i in range(number_of - 1) if counts[i] < limit]
        pool, remaining = sum([weights[i] for i in movable]), rest
        for i in movable:
            addition = min(limit - counts[i], max(1, remaining * weights[i] // pool), rest)
            counts[i] = counts[i] + addition
            rest = rest - addition
    return np.array([limit] + counts)


def uneven_parts(rng, amount, total, most, skew):
    if amount == 2:
        one = jax.random.randint(rng, (), max(1, total - most), min(most, total - 1) + 1)
        return jnp.stack([one, total - one])
    tallies = jnp.asarray(length_profile(amount, total, most, skew), jnp.int32)
    couples = (amount - 1) // 2
    source_of, sink = tallies[1:1 + 2 * couples:2], tallies[2:2 + 2 * couples:2]
    room = jnp.minimum(source_of - 1, most - sink)
    passed = jax.random.randint(jax.random.fold_in(rng, 1), (couples,), 0, 1 << 20) % (room + 1)
    tallies = tallies.at[1:1 + 2 * couples:2].set(source_of - passed).at[2:2 + 2 * couples:2].set(sink + passed)
    return tallies[jax.random.permutation(jax.random.fold_in(rng, 2), amount)]


def bell_draw(own_key, shape, spread, limit, pieces=(), held_as=jnp.bfloat16):
    loudness = steps_of(own_key, shape, pieces, -0.22, 0.18) if pieces else 1.0
    array = jax.random.normal(own_key, shape, jnp.float32) * spread * loudness
    return jnp.minimum(jnp.maximum(array, -limit), limit).astype(held_as)


def setup_inputs(seed: int = 0) -> dict:
    keys = jax.random.split(jax.random.key(seed), 9)
    hidden = draw_hidden(jax.random.fold_in(keys[8], 71), 0)
    lengths = jax.vmap(lambda own: uneven_parts(own, CAND, LIST_LEN, MOST, 2))(jax.random.split(keys[1], LISTS)).reshape((LISTS, CAND)).astype(jnp.int32)
    ranks = jax.vmap(lambda own: jax.random.permutation(own, CAND))(jax.random.split(keys[2], LISTS)).reshape((LISTS, CAND)).astype(jnp.int32)
    gain = jnp.clip(1.0 + 0.1 * jax.random.normal(keys[3], (D,), jnp.float32), 0.5, 1.5).astype(jnp.bfloat16)
    head = draw_head(jax.random.fold_in(keys[8], 71), 0)
    local_frag = bell_draw(keys[5], (N_REP, FROWS, D), 1.0, 6.0, ((0, 32), (1, 8)))
    global_prev = bell_draw(keys[6], (FROWS, D), 0.5, 4.0, ((0, 8),), jnp.float32)
    momentum = bell_draw(keys[7], (FROWS, D), 0.3, 3.0, ((0, 8),), jnp.float32)
    return {"hidden": hidden, "lengths": lengths, "ranks": ranks, "gain": gain, "head": head, "local_frag": local_frag, "global_prev": global_prev, "momentum": momentum}


SOFTCAP = 30.0
TEMPER = 2.0
LOSS_SCALE = 512.0
OUTER_RATE = 0.7
MOMENTUM = 0.9
MIXING = 0.5
EPSILON = 1e-06

def membership(lengths, list_len):
    ends = jnp.cumsum(lengths, axis=-1).astype(jnp.int32)
    starts = (ends - lengths).astype(jnp.int32)
    position = jnp.arange(list_len, dtype=jnp.int32)
    inside = (position[None, None, :] >= starts[:, :, None]) & (position[None, None, :] < ends[:, :, None])
    return inside.astype(jnp.float32)

def head_pass(hidden_lists, lengths, ranks, gain, head):
    member = membership(lengths, hidden_lists.shape[1])
    values = hidden_lists.astype(jnp.float32)
    inverse = lax.rsqrt(lax.optimization_barrier(jnp.mean(values * values, axis=-1, keepdims=True)) + EPSILON)
    normal = values * inverse
    gain_wide = gain.astype(jnp.float32)
    head_wide = head.astype(jnp.float32)
    normed = normal * gain_wide
    root = jnp.sqrt(lengths.astype(jnp.float32))
    pooled = jnp.einsum('lct,ltd->lcd', member, normed, precision=lax.Precision.HIGHEST) / root[:, :, None]
    raw = jnp.einsum('lcd,d->lc', pooled, head_wide, precision=lax.Precision.HIGHEST)
    capped = SOFTCAP * jnp.tanh(raw / SOFTCAP)
    weights = jnp.exp(capped)
    probs = weights / lax.optimization_barrier(jnp.sum(weights, axis=-1, keepdims=True))
    teacher = jnp.exp(-ranks.astype(jnp.float32) / TEMPER)
    target = teacher / lax.optimization_barrier(jnp.sum(teacher, axis=-1, keepdims=True))
    slope = LOSS_SCALE * (probs - target) * (1.0 - (capped / SOFTCAP) ** 2)
    dpooled = slope[:, :, None] * head_wide[None, None, :] / root[:, :, None]
    dnormed = jnp.einsum('lct,lcd->ltd', member, dpooled, precision=lax.Precision.HIGHEST)
    grad_gain = lax.optimization_barrier(jnp.sum(dnormed * normal, axis=(0, 1))) / LOSS_SCALE
    grad_head = jnp.einsum('lc,lcd->d', slope, pooled, precision=lax.Precision.HIGHEST) / LOSS_SCALE
    dnormal = dnormed * gain_wide
    dvalues = inverse * (dnormal - normal * lax.optimization_barrier(jnp.mean(dnormal * normal, axis=-1, keepdims=True)))
    return (dvalues.astype(jnp.bfloat16), grad_gain, grad_head)

def reference(hidden, lengths, ranks, gain, head, local_frag, global_prev, momentum):
    lists_rep = hidden.shape[0] // N_REP // LIST_LEN
    hidden_rep = hidden.reshape(N_REP, lists_rep, LIST_LEN, D)
    lengths_rep = lengths.reshape(N_REP, lists_rep, CAND)
    ranks_rep = ranks.reshape(N_REP, lists_rep, CAND)

    def one_replica(items):
        return head_pass(items[0], items[1], items[2], gain, head)
    d_rep, grad_gain, grad_head = lax.map(one_replica, (hidden_rep, lengths_rep, ranks_rep))
    d_hidden = d_rep.reshape(hidden.shape)
    local_wide = local_frag.astype(jnp.float32)
    outer = global_prev[None, :, :] - local_wide
    average = lax.optimization_barrier(jnp.sum(outer, axis=0)) / N_REP
    new_momentum = MOMENTUM * momentum + average
    new_global = global_prev - OUTER_RATE * (MOMENTUM * new_momentum + average)
    merged = (MIXING * local_wide + (1.0 - MIXING) * new_global[None, :, :]).astype(jnp.bfloat16)
    return (d_hidden, grad_gain, grad_head, new_global, new_momentum, merged)
```

```python
import jax
import jax.numpy as jnp
from jax import lax
from jax.experimental import pallas as pl
from jax.experimental.pallas import tpu as pltpu
from jax.sharding import PartitionSpec as P

LIST_LEN = 256
CAND = 8
LANES = 128
ROWS = 32

SOFTCAP = 30.0
TEMPER = 2.0
LOSS_SCALE = 512.0
OUTER_RATE = 0.7
MOMENTUM = 0.9
MIXING = 0.5
EPSILON = 1e-06

PLANES = 2
PLANE = 16


def head_kernel(lengths_ref, ranks_ref, hidden_ref, v_ref, out_ref, w_ref, square_ref, dot_ref):
    tokens, width = hidden_ref.shape

    def first(step, carry):
        rows = pl.ds(pl.multiple_of(step * ROWS, ROWS), ROWS)
        values = hidden_ref[rows, :].astype(jnp.float32)
        square_ref[rows, :] = jnp.sum(values * values, axis=1, keepdims=True)
        dot_ref[rows, :] = jnp.sum(values * v_ref[...], axis=1, keepdims=True)
        return carry

    lax.fori_loop(0, tokens // ROWS, first, 0)

    inverse = lax.rsqrt(square_ref[...] / width + EPSILON)
    dots = dot_ref[...]

    lane = lax.broadcasted_iota(jnp.int32, (1, LANES), 1)
    starts = jnp.zeros((1, LANES), jnp.int32)
    ends = jnp.zeros((1, LANES), jnp.int32)
    ranks = jnp.zeros((1, LANES), jnp.int32)
    end = jnp.int32(0)
    for c in range(CAND):
        start, end = end, end + lengths_ref[0, c]
        starts = jnp.where(lane == c, start, starts)
        ends = jnp.where(lane == c, end, ends)
        ranks = jnp.where(lane == c, ranks_ref[0, c], ranks)
    real = lane < CAND
    root = jnp.sqrt(jnp.where(real, ends - starts, 1).astype(jnp.float32))
    position = lax.broadcasted_iota(jnp.int32, (tokens, LANES), 0)
    member = (position >= starts) & (position < ends)

    raw = jnp.sum(jnp.where(member, inverse * dots, 0.0), axis=0, keepdims=True) / root
    capped = SOFTCAP * jnp.tanh(raw / SOFTCAP)
    weights = jnp.where(real, jnp.exp(capped), 0.0)
    probs = weights / jnp.sum(weights, axis=1, keepdims=True)
    teacher = jnp.where(real, jnp.exp(-ranks.astype(jnp.float32) / TEMPER), 0.0)
    target = teacher / jnp.sum(teacher, axis=1, keepdims=True)
    slope = LOSS_SCALE * (probs - target) * (1.0 - (capped / SOFTCAP) ** 2)
    scale = jnp.sum(jnp.where(member, slope / root, 0.0), axis=1, keepdims=True)

    alpha = inverse * scale
    square_ref[...] = alpha
    dot_ref[...] = alpha * inverse * inverse * dots / width
    w_ref[...] = jnp.zeros_like(w_ref)

    def second(step, carry):
        rows = pl.ds(pl.multiple_of(step * ROWS, ROWS), ROWS)
        values = hidden_ref[rows, :].astype(jnp.float32)
        alphas = square_ref[rows, :]
        out_ref[rows, :] = (alphas * v_ref[...] - dot_ref[rows, :] * values).astype(out_ref.dtype)
        w_ref[...] += jnp.sum(alphas * values, axis=0, keepdims=True)
        return carry

    lax.fori_loop(0, tokens // ROWS, second, 0)
    w_ref[...] = w_ref[...] / LOSS_SCALE


def head_call(hidden, lengths, ranks, v):
    tokens, width = hidden.shape
    smem = pl.BlockSpec(memory_space=pltpu.SMEM)
    vmem = pl.BlockSpec(memory_space=pltpu.VMEM)
    return pl.pallas_call(
        head_kernel,
        out_shape=(
            jax.ShapeDtypeStruct((tokens, width), jnp.bfloat16),
            jax.ShapeDtypeStruct((1, width), jnp.float32),
        ),
        in_specs=[smem, smem, vmem, vmem],
        out_specs=(vmem, vmem),
        scratch_shapes=[pltpu.VMEM((tokens, 1), jnp.float32), pltpu.VMEM((tokens, 1), jnp.float32)],
        compiler_params=pltpu.CompilerParams(vmem_limit_bytes=24 * 1024 * 1024),
        cost_estimate=pl.CostEstimate(flops=10 * tokens * width, bytes_accessed=4 * tokens * width, transcendentals=0),
        name="head",
    )(lengths, ranks, hidden, v)


def head_work(hidden, lengths, ranks, gain, head):
    devices = lax.axis_size("fsdp")
    gain_wide, head_wide = gain.astype(jnp.float32), head.astype(jnp.float32)
    own = gain_wide * head_wide
    v = lax.all_to_all(
        jnp.broadcast_to(own[None, :], (devices, own.shape[0])), "fsdp", 0, 0, tiled=True
    ).reshape(1, hidden.shape[1])
    d_hidden, w = head_call(hidden, lengths, ranks, v)
    w = lax.all_to_all(w.reshape(devices, own.shape[0]), "fsdp", 0, 0, tiled=True)
    w = jnp.sum(w, axis=0)
    return d_hidden, (w * head_wide)[None, :], (w * gain_wide)[None, :]


def outer_work(local_frag, global_prev, momentum):
    rows, width = global_prev.shape
    replicas = lax.axis_size("rep")
    planes = [[PLANE * z + i for i in range(PLANE)] for z in range(PLANES)]
    other_plane = [(i, (i + PLANE) % replicas) for i in range(replicas)]
    piece = rows // PLANE
    local = local_frag[0]
    mine = lax.all_to_all(
        local.reshape(PLANE, piece, width), "rep", 0, 0, tiled=True, axis_index_groups=planes
    )
    partial = jnp.sum(mine.astype(jnp.float32), axis=0)
    total = partial + lax.ppermute(partial, "rep", other_plane)
    at = lax.rem(lax.axis_index("rep"), PLANE) * piece
    average = lax.dynamic_slice_in_dim(global_prev, at, piece, 0) - total / replicas
    average = lax.all_to_all(
        jnp.broadcast_to(average[None], (PLANE, piece, width)), "rep", 0, 0, tiled=True, axis_index_groups=planes
    ).reshape(rows, width)
    new_momentum = MOMENTUM * momentum + average
    new_global = global_prev - OUTER_RATE * (MOMENTUM * new_momentum + average)
    merged = (MIXING * local.astype(jnp.float32) + (1.0 - MIXING) * new_global).astype(jnp.bfloat16)
    return new_global, new_momentum, merged[None]


def body(hidden, lengths, ranks, gain, head, local_frag, global_prev, momentum):
    d_hidden, grad_gain, grad_head = head_work(hidden, lengths, ranks, gain, head)
    new_global, new_momentum, merged = outer_work(local_frag, global_prev, momentum)
    return d_hidden, grad_gain, grad_head, new_global, new_momentum, merged


def solution(mesh):
    placed = (
        P(("rep", "fsdp"), None),
        P(("rep", "fsdp"), None),
        P(("rep", "fsdp"), None),
        P("fsdp"),
        P("fsdp"),
        P("rep", "fsdp", None),
        P("fsdp", None),
        P("fsdp", None),
    )
    return jax.shard_map(
        body,
        mesh=mesh,
        in_specs=placed,
        out_specs=(
            P(("rep", "fsdp"), None),
            P("rep", "fsdp"),
            P("rep", "fsdp"),
            P("fsdp", None),
            P("fsdp", None),
            P("rep", "fsdp", None),
        ),
        check_vma=False,
    )
```

```python
import jax
import jax.numpy as jnp
from jax import lax
from jax.experimental import pallas as pl
from jax.experimental.pallas import tpu as pltpu
from jax.sharding import PartitionSpec as P

LIST_LEN = 256
CAND = 8
LANES = 128
ROWS = 32

SOFTCAP = 30.0
TEMPER = 2.0
LOSS_SCALE = 512.0
OUTER_RATE = 0.7
MOMENTUM = 0.9
MIXING = 0.5
EPSILON = 1e-06

PLANES = 2
PLANE = 16


def score_kernel(place_ref, lengths_ref, ranks_ref, hidden_ref, own_ref, one_ref, two_ref, three_ref,
                 w_ref, alpha_ref, beta_ref, v_ref, scale_ref):
    tokens, width = hidden_ref.shape
    block = own_ref.shape[1]
    place = place_ref[0, 0]
    columns = [pl.ds(pl.multiple_of((place ^ k) * block, LANES), block) for k in range(4)]
    for part, ref in zip(columns, (own_ref, one_ref, two_ref, three_ref)):
        v_ref[:, part] = ref[...]

    def first(step, carry):
        rows = pl.ds(pl.multiple_of(step * ROWS, ROWS), ROWS)
        square = jnp.zeros((ROWS, LANES), jnp.float32)
        dot = jnp.zeros((ROWS, LANES), jnp.float32)
        for j in range(width // LANES):
            part = slice(j * LANES, (j + 1) * LANES)
            values = hidden_ref[rows, part].astype(jnp.float32)
            square += values * values
            dot += values * v_ref[:, part]
        alpha_ref[rows, :] = jnp.sum(square, axis=1, keepdims=True)
        beta_ref[rows, :] = jnp.sum(dot, axis=1, keepdims=True)
        return carry

    lax.fori_loop(0, tokens // ROWS, first, 0)

    inverse = lax.rsqrt(alpha_ref[...] / width + EPSILON)
    dots = beta_ref[...]

    lane = lax.broadcasted_iota(jnp.int32, (1, LANES), 1)
    starts = jnp.zeros((1, LANES), jnp.int32)
    ends = jnp.zeros((1, LANES), jnp.int32)
    ranks = jnp.zeros((1, LANES), jnp.int32)
    end = jnp.int32(0)
    for c in range(CAND):
        start, end = end, end + lengths_ref[0, c]
        starts = jnp.where(lane == c, start, starts)
        ends = jnp.where(lane == c, end, ends)
        ranks = jnp.where(lane == c, ranks_ref[0, c], ranks)
    real = lane < CAND
    root = jnp.sqrt(jnp.where(real, ends - starts, 1).astype(jnp.float32))
    position = lax.broadcasted_iota(jnp.int32, (tokens, LANES), 0)
    member = (position >= starts) & (position < ends)

    raw = jnp.sum(jnp.where(member, inverse * dots, 0.0), axis=0, keepdims=True) / root
    capped = SOFTCAP * jnp.tanh(raw / SOFTCAP)
    weights = jnp.where(real, jnp.exp(capped), 0.0)
    probs = weights / jnp.sum(weights, axis=1, keepdims=True)
    teacher = jnp.where(real, jnp.exp(-ranks.astype(jnp.float32) / TEMPER), 0.0)
    target = teacher / jnp.sum(teacher, axis=1, keepdims=True)
    slope = LOSS_SCALE * (probs - target) * (1.0 - (capped / SOFTCAP) ** 2)
    scale = jnp.sum(jnp.where(member, slope / root, 0.0), axis=1, keepdims=True)

    alpha = inverse * scale
    alpha_ref[...] = alpha
    beta_ref[...] = alpha * inverse * inverse * dots / width
    scale_ref[...] = jnp.broadcast_to(alpha, scale_ref.shape)

    for k, columns_k in enumerate(columns):
        for j in range(block // LANES):
            at = pl.multiple_of((place ^ k) * block + j * LANES, LANES)
            total = jnp.zeros((ROWS, LANES), jnp.float32)
            for row in range(0, tokens, ROWS):
                values = hidden_ref[row:row + ROWS, pl.ds(at, LANES)].astype(jnp.float32)
                total += values * scale_ref[row:row + ROWS, :]
            w_ref[k:k + 1, j * LANES:(j + 1) * LANES] = jnp.sum(total, axis=0, keepdims=True) / LOSS_SCALE


def score_call(place, lengths, ranks, hidden, blocks):
    tokens, width = hidden.shape
    block = width // 4
    smem = pl.BlockSpec(memory_space=pltpu.SMEM)
    vmem = pl.BlockSpec(memory_space=pltpu.VMEM)
    column = jax.ShapeDtypeStruct((tokens, 1), jnp.float32)
    return pl.pallas_call(
        score_kernel,
        out_shape=(jax.ShapeDtypeStruct((4, block), jnp.float32), column, column,
                   jax.ShapeDtypeStruct((1, width), jnp.float32)),
        in_specs=[smem, smem, smem, vmem, vmem, vmem, vmem, vmem],
        out_specs=(vmem, vmem, vmem, vmem),
        scratch_shapes=[pltpu.VMEM((tokens, LANES), jnp.float32)],
        compiler_params=pltpu.CompilerParams(vmem_limit_bytes=16 * 1024 * 1024),
        cost_estimate=pl.CostEstimate(flops=6 * tokens * width, bytes_accessed=2 * tokens * width, transcendentals=0),
        name="score",
    )(place, lengths, ranks, hidden, *blocks)


def token_kernel(hidden_ref, v_ref, alpha_ref, beta_ref, out_ref):
    for j in range(hidden_ref.shape[1] // LANES):
        part = slice(j * LANES, (j + 1) * LANES)
        values = hidden_ref[:, part].astype(jnp.float32)
        out_ref[:, part] = (alpha_ref[...] * v_ref[:, part] - beta_ref[...] * values).astype(out_ref.dtype)


def token_call(hidden, v, alpha, beta):
    tokens, width = hidden.shape
    step = 64
    return pl.pallas_call(
        token_kernel,
        grid=(tokens // step,),
        out_shape=jax.ShapeDtypeStruct((tokens, width), jnp.bfloat16),
        in_specs=[
            pl.BlockSpec((step, width), lambda i: (i, 0)),
            pl.BlockSpec((1, width), lambda i: (0, 0)),
            pl.BlockSpec((step, 1), lambda i: (i, 0)),
            pl.BlockSpec((step, 1), lambda i: (i, 0)),
        ],
        out_specs=pl.BlockSpec((step, width), lambda i: (i, 0)),
        compiler_params=pltpu.CompilerParams(vmem_limit_bytes=16 * 1024 * 1024),
        cost_estimate=pl.CostEstimate(flops=4 * tokens * width, bytes_accessed=4 * tokens * width, transcendentals=0),
        name="token_grad",
    )(hidden, v, alpha, beta)


def along(array, k):
    devices = lax.axis_size("fsdp")
    return lax.ppermute(array, "fsdp", [(i, i ^ k) for i in range(devices)])


def outer_reduce(local):
    rows, width = local.shape
    planes = [[PLANE * z + i for i in range(PLANE)] for z in range(PLANES)]
    return lax.all_to_all(
        local.reshape(PLANE, rows // PLANE, width), "rep", 0, 0, tiled=True, axis_index_groups=planes
    )


def outer_average(total, global_prev):
    piece = total.shape[0]
    at = lax.rem(lax.axis_index("rep"), PLANE) * piece
    return lax.dynamic_slice_in_dim(global_prev, at, piece, 0) - total / lax.axis_size("rep")


def outer_spread(average):
    planes = [[PLANE * z + i for i in range(PLANE)] for z in range(PLANES)]
    sent = jnp.broadcast_to(average.astype(jnp.float16)[None], (PLANE, *average.shape))
    return sent, lambda sent: lax.all_to_all(sent, "rep", 0, 0, tiled=True, axis_index_groups=planes)


def outer_update(average, global_prev, momentum, local):
    new_momentum = MOMENTUM * momentum + average
    new_global = global_prev - OUTER_RATE * (MOMENTUM * new_momentum + average)
    merged = (MIXING * local.astype(jnp.float32) + (1.0 - MIXING) * new_global).astype(jnp.bfloat16)
    return new_global, new_momentum, merged[None]


def body(hidden, lengths, ranks, gain, head, local_frag, global_prev, momentum):
    barrier = lax.optimization_barrier
    replicas = lax.axis_size("rep")
    here = lax.axis_index("fsdp")
    core, place = here % 2, here // 2
    gain_wide, head_wide = gain.astype(jnp.float32)[None], head.astype(jnp.float32)[None]
    local = local_frag[0]

    mine = outer_reduce(local)

    own = gain_wide * head_wide
    twin = along(own, 1)
    pair = jnp.where(core == 0, jnp.concatenate([own, twin], 1), jnp.concatenate([twin, own], 1))
    blocks = (pair, along(pair, 2), along(pair, 4), along(pair, 6))

    mine, blocks = barrier((mine, blocks))
    partial = jnp.sum(mine.astype(jnp.float32), axis=0)
    partial, blocks = barrier((partial, blocks))
    far = lax.ppermute(partial, "rep", [(i, (i + PLANE) % replicas) for i in range(replicas)])

    w, alpha, beta, v = score_call(place.astype(jnp.int32).reshape(1, 1), lengths, ranks, hidden, blocks)
    far, w, alpha, beta, v = barrier((far, w, alpha, beta, v))

    sent, spread = outer_spread(outer_average(partial + far, global_prev))
    sent, w, alpha = barrier((sent, w, alpha))
    average = spread(sent)

    w = w[0:1] + along(w[1:2], 2) + along(w[2:3], 4) + along(w[3:4], 6)
    half = own.shape[1]
    low, high = w[:, :half], w[:, half:]
    w = jnp.where(core == 0, low, high) + along(jnp.where(core == 0, high, low), 1)
    d_hidden = token_call(hidden, v, alpha, beta)

    new_global, new_momentum, merged = outer_update(
        average.reshape(global_prev.shape).astype(jnp.float32), global_prev, momentum, local
    )
    return d_hidden, w * head_wide, w * gain_wide, new_global, new_momentum, merged


def solution(mesh):
    placed = (
        P(("rep", "fsdp"), None),
        P(("rep", "fsdp"), None),
        P(("rep", "fsdp"), None),
        P("fsdp"),
        P("fsdp"),
        P("rep", "fsdp", None),
        P("fsdp", None),
        P("fsdp", None),
    )
    return jax.shard_map(
        body,
        mesh=mesh,
        in_specs=placed,
        out_specs=(
            P(("rep", "fsdp"), None),
            P("rep", "fsdp"),
            P("rep", "fsdp"),
            P("fsdp", None),
            P("fsdp", None),
            P("rep", "fsdp", None),
        ),
        check_vma=False,
    )
```

```python
import jax
import jax.numpy as jnp
from jax import lax
from jax.experimental import pallas as pl
from jax.experimental.pallas import tpu as pltpu
from jax.sharding import PartitionSpec as P

LIST_LEN = 256
CAND = 8
LANES = 128
ROWS = 32

SOFTCAP = 30.0
TEMPER = 2.0
LOSS_SCALE = 512.0
OUTER_RATE = 0.7
MOMENTUM = 0.9
MIXING = 0.5
EPSILON = 1e-06

PLANES = 2
PLANE = 16
TALL, BROAD = 16, 1152
LARGEST = 10.0
STEPS = 32767.0
SHARES = 4
VMEM_LIMIT = 16 * 1024 * 1024


def score_kernel(lengths_ref, ranks_ref, hidden_ref, v_ref, alpha_ref, beta_ref, square_ref, dot_ref):
    tokens, width = hidden_ref.shape

    def first(step, carry):
        rows = pl.ds(pl.multiple_of(step * ROWS, ROWS), ROWS)
        square = jnp.zeros((ROWS, LANES), jnp.float32)
        dot = jnp.zeros((ROWS, LANES), jnp.float32)
        for j in range(width // LANES):
            part = slice(j * LANES, (j + 1) * LANES)
            values = hidden_ref[rows, part].astype(jnp.float32)
            square += values * values
            dot += values * v_ref[:, part]
        square_ref[rows, :] = jnp.sum(square, axis=1, keepdims=True)
        dot_ref[rows, :] = jnp.sum(dot, axis=1, keepdims=True)
        return carry

    lax.fori_loop(0, tokens // ROWS, first, 0)

    inverse = lax.rsqrt(square_ref[...] / width + EPSILON)
    dots = dot_ref[...]

    lane = lax.broadcasted_iota(jnp.int32, (1, LANES), 1)
    starts = jnp.zeros((1, LANES), jnp.int32)
    ends = jnp.zeros((1, LANES), jnp.int32)
    ranks = jnp.zeros((1, LANES), jnp.int32)
    end = jnp.int32(0)
    for c in range(CAND):
        start, end = end, end + lengths_ref[0, c]
        starts = jnp.where(lane == c, start, starts)
        ends = jnp.where(lane == c, end, ends)
        ranks = jnp.where(lane == c, ranks_ref[0, c], ranks)
    real = lane < CAND
    root = jnp.sqrt(jnp.where(real, ends - starts, 1).astype(jnp.float32))
    position = lax.broadcasted_iota(jnp.int32, (tokens, LANES), 0)
    member = (position >= starts) & (position < ends)

    raw = jnp.sum(jnp.where(member, inverse * dots, 0.0), axis=0, keepdims=True) / root
    capped = SOFTCAP * jnp.tanh(raw / SOFTCAP)
    weights = jnp.where(real, jnp.exp(capped), 0.0)
    probs = weights / jnp.sum(weights, axis=1, keepdims=True)
    teacher = jnp.where(real, jnp.exp(-ranks.astype(jnp.float32) / TEMPER), 0.0)
    target = teacher / jnp.sum(teacher, axis=1, keepdims=True)
    slope = LOSS_SCALE * (probs - target) * (1.0 - (capped / SOFTCAP) ** 2)
    scale = jnp.sum(jnp.where(member, slope / root, 0.0), axis=1, keepdims=True)

    alpha = inverse * scale
    alpha_ref[...] = jnp.broadcast_to(alpha, alpha_ref.shape)
    beta_ref[...] = jnp.broadcast_to(alpha * inverse * inverse * dots / width, beta_ref.shape)


def score_call(lengths, ranks, hidden, v):
    tokens, width = hidden.shape
    smem = pl.BlockSpec(memory_space=pltpu.SMEM)
    vmem = pl.BlockSpec(memory_space=pltpu.VMEM)
    wide = jax.ShapeDtypeStruct((tokens, LANES), jnp.float32)
    return pl.pallas_call(
        score_kernel,
        out_shape=(wide, wide),
        in_specs=[smem, smem, vmem, vmem],
        out_specs=(vmem, vmem),
        scratch_shapes=[pltpu.VMEM((tokens, 1), jnp.float32)] * 2,
        compiler_params=pltpu.CompilerParams(vmem_limit_bytes=VMEM_LIMIT),
        cost_estimate=pl.CostEstimate(flops=4 * tokens * width, bytes_accessed=2 * tokens * width, transcendentals=0),
        name="score",
    )(lengths, ranks, hidden, v)


def weigh_kernel(hidden_ref, alpha_ref, mark_ref, w_ref):
    tokens, width = hidden_ref.shape
    for j in range(width // LANES):
        part = slice(j * LANES, (j + 1) * LANES)
        total = jnp.zeros((ROWS, LANES), jnp.float32)
        for row in range(0, tokens, ROWS):
            rows = slice(row, row + ROWS)
            total += alpha_ref[rows, :] * hidden_ref[rows, part].astype(jnp.float32)
        w_ref[:, part] = jnp.sum(total, axis=0, keepdims=True) * (1.0 / LOSS_SCALE)


def weigh_call(hidden, alpha, mark):
    tokens, width = hidden.shape
    vmem = pl.BlockSpec(memory_space=pltpu.VMEM)
    return pl.pallas_call(
        weigh_kernel,
        out_shape=jax.ShapeDtypeStruct((1, width), jnp.float32),
        in_specs=[vmem] * 3,
        out_specs=vmem,
        compiler_params=pltpu.CompilerParams(vmem_limit_bytes=VMEM_LIMIT),
        cost_estimate=pl.CostEstimate(flops=2 * tokens * width, bytes_accessed=2 * tokens * width, transcendentals=0),
        name="weigh",
    )(hidden, alpha, mark)


def token_kernel(hidden_ref, v_ref, alpha_ref, beta_ref, out_ref, kept_ref, sem):
    tokens, width = hidden_ref.shape
    copies = []
    for band in range(width // BROAD):
        for j in range(BROAD // LANES):
            part = slice(band * BROAD + j * LANES, band * BROAD + (j + 1) * LANES)
            v = v_ref[:, part]
            for row in range(0, tokens, ROWS):
                rows = slice(row, row + ROWS)
                values = hidden_ref[rows, part].astype(jnp.float32)
                kept_ref[rows, part] = (alpha_ref[rows, :] * v - beta_ref[rows, :] * values).astype(kept_ref.dtype)
        columns = slice(band * BROAD, (band + 1) * BROAD)
        copies.append(pltpu.make_async_copy(kept_ref.at[:, columns], out_ref.at[:, columns], sem.at[band]))
        copies[-1].start()
    for copy in copies:
        copy.wait()


def token_call(hidden, v, alpha, beta):
    tokens, width = hidden.shape
    vmem = pl.BlockSpec(memory_space=pltpu.VMEM)
    return pl.pallas_call(
        token_kernel,
        out_shape=jax.ShapeDtypeStruct((tokens, width), jnp.bfloat16),
        in_specs=[vmem] * 4,
        out_specs=pl.BlockSpec(memory_space=pl.ANY),
        scratch_shapes=[pltpu.VMEM((tokens, width), jnp.bfloat16), pltpu.SemaphoreType.DMA((width // BROAD,))],
        compiler_params=pltpu.CompilerParams(vmem_limit_bytes=VMEM_LIMIT),
        cost_estimate=pl.CostEstimate(flops=6 * tokens * width, bytes_accessed=4 * tokens * width, transcendentals=0),
        name="token_grad",
    )(hidden, v, alpha, beta)


def along(array, k):
    devices = lax.axis_size("fsdp")
    return lax.ppermute(array, "fsdp", [(i, i ^ k) for i in range(devices)])


def average_kernel(near_ref, far_ref, global_ref, out_ref, mark_ref, coded_ref, sem):
    average = global_ref[...] - (near_ref[...] + far_ref[...]) * (1.0 / (PLANES * PLANE))
    top = jnp.max(jnp.abs(average), axis=1, keepdims=True)
    unit = jnp.clip(jnp.ceil(top * (STEPS / LARGEST)), 1.0, STEPS)
    steps = jnp.clip(jnp.floor(average * ((STEPS * STEPS / LARGEST) / unit) + 0.5), -STEPS, STEPS)
    copies = []
    for part in range(SHARES):
        coded_ref[part, :, :BROAD] = steps.astype(jnp.int32).astype(coded_ref.dtype)
        coded_ref[part, :, BROAD:] = jnp.broadcast_to(unit, (TALL, LANES)).astype(jnp.int32).astype(coded_ref.dtype)
    for part in range(PLANE // SHARES):
        copies.append(pltpu.make_async_copy(coded_ref, out_ref.at[pl.ds(part * SHARES, SHARES)], sem.at[part]))
    mark_ref[...] = jnp.zeros_like(mark_ref)
    for copy in copies:
        copy.start()
    for copy in copies:
        copy.wait()


def average_call(near, far, own_global):
    vmem = pl.BlockSpec(memory_space=pltpu.VMEM)
    return pl.pallas_call(
        average_kernel,
        out_shape=(jax.ShapeDtypeStruct((PLANE, TALL, BROAD + LANES), jnp.int16), jax.ShapeDtypeStruct((1, LANES), jnp.float32)),
        in_specs=[vmem, vmem, vmem],
        out_specs=(pl.BlockSpec(memory_space=pl.ANY), vmem),
        scratch_shapes=[pltpu.VMEM((SHARES, TALL, BROAD + LANES), jnp.int16), pltpu.SemaphoreType.DMA((PLANE // SHARES,))],
        compiler_params=pltpu.CompilerParams(vmem_limit_bytes=VMEM_LIMIT),
        cost_estimate=pl.CostEstimate(flops=10 * near.size, bytes_accessed=40 * near.size, transcendentals=0),
        name="average",
    )(near, far, own_global)


def update_kernel(coded_ref, w_ref, gain_ref, head_ref, global_ref, momentum_ref, local_ref,
                  grad_gain_ref, grad_head_ref, *refs):
    outs, kept, sem = refs[:3], refs[3:6], refs[6]
    rows, width = global_ref.shape
    across = width // BROAD
    new_global_ref, new_momentum_ref, merged_ref = kept
    copies = []
    for band in range(rows // TALL):
        row = slice(band * TALL, (band + 1) * TALL)
        for column in range(across):
            p = band * across + column
            scale = coded_ref[p, :, BROAD:].astype(jnp.int32).astype(jnp.float32) * (LARGEST / (STEPS * STEPS))
            for j in range(BROAD // LANES):
                part = slice(column * BROAD + j * LANES, column * BROAD + (j + 1) * LANES)
                steps = coded_ref[p, :, j * LANES:(j + 1) * LANES].astype(jnp.int32).astype(jnp.float32)
                average = steps * scale
                new_momentum = MOMENTUM * momentum_ref[row, part] + average
                new_global = global_ref[row, part] - OUTER_RATE * (MOMENTUM * new_momentum + average)
                new_momentum_ref[row, part] = new_momentum
                new_global_ref[row, part] = new_global
                merged = MIXING * local_ref[row, part].astype(jnp.float32) + (1.0 - MIXING) * new_global
                merged_ref[row, part] = merged.astype(merged_ref.dtype)
        for n in range(3):
            copies.append(pltpu.make_async_copy(kept[n].at[row, :], outs[n].at[row, :], sem.at[n, band]))
            copies[-1].start()
    w = w_ref[...]
    grad_gain_ref[...] = w * head_ref[...]
    grad_head_ref[...] = w * gain_ref[...]
    for copy in copies:
        copy.wait()


def update_call(coded, w, gain, head, global_prev, momentum, local):
    rows, width = global_prev.shape
    vmem = pl.BlockSpec(memory_space=pltpu.VMEM)
    whole = pl.BlockSpec(memory_space=pl.ANY)
    wide, narrow = jnp.float32, jnp.bfloat16
    grad = jax.ShapeDtypeStruct(w.shape, wide)
    return pl.pallas_call(
        update_kernel,
        out_shape=(grad, grad) + tuple(jax.ShapeDtypeStruct((rows, width), t) for t in (wide, wide, narrow)),
        in_specs=[vmem] * 7,
        out_specs=(vmem,) * 2 + (whole,) * 3,
        scratch_shapes=[pltpu.VMEM((rows, width), t) for t in (wide, wide, narrow)]
        + [pltpu.SemaphoreType.DMA((3, rows // TALL))],
        compiler_params=pltpu.CompilerParams(vmem_limit_bytes=VMEM_LIMIT),
        cost_estimate=pl.CostEstimate(flops=10 * rows * width, bytes_accessed=22 * rows * width, transcendentals=0),
        name="update",
    )(coded, w, gain, head, global_prev, momentum, local)


def body(hidden, lengths, ranks, gain, head, local_frag, global_prev, momentum):
    barrier = lax.optimization_barrier
    replicas, devices = lax.axis_size("rep"), lax.axis_size("fsdp")
    planes = [[PLANE * z + i for i in range(PLANE)] for z in range(PLANES)]
    here = lax.axis_index("fsdp")
    local = local_frag[0]

    pieces = local.reshape(4, TALL, 4, BROAD).transpose(0, 2, 1, 3).reshape(PLANE, TALL, BROAD)
    pieces, gain, head = barrier((pieces, gain, head))
    gain_wide, head_wide = gain.astype(jnp.float32)[None], head.astype(jnp.float32)[None]
    mine = lax.all_to_all(pieces, "rep", 0, 0, tiled=True, axis_index_groups=planes)

    v = gain_wide * head_wide
    for bit in (1, 2, 4):
        other = along(v, bit)
        v = jnp.where(here & bit == 0, jnp.concatenate([v, other], 1), jnp.concatenate([other, v], 1))
    owned = lax.rem(lax.axis_index("rep"), PLANE)
    across = global_prev.shape[1] // BROAD
    own_global = lax.dynamic_slice(global_prev, (owned // across * TALL, owned % across * BROAD), (TALL, BROAD))

    mine, own_global = barrier((mine, own_global))
    near = jnp.sum(mine.astype(jnp.float32), axis=0)
    far = lax.ppermute(near, "rep", [(i, (i + PLANE) % replicas) for i in range(replicas)])

    alpha, beta = score_call(lengths, ranks, hidden, v)
    far, alpha, beta = barrier((far, alpha, beta))

    coded, mark = average_call(near, far, own_global)
    received = lax.all_to_all(coded, "rep", 0, 0, tiled=True, axis_index_groups=planes)

    def halve(hidden, v, alpha, beta, w):
        d_hidden = None
        for bit in (4, 2, 1):
            half = w.shape[1] // 2
            low, high = w[:, :half], w[:, half:]
            kept, sent = jnp.where(here & bit == 0, low, high), jnp.where(here & bit == 0, high, low)
            term = along(sent, bit)
            if bit == 4:
                d_hidden = token_call(hidden, v, alpha, beta)
                term, d_hidden = barrier((term, d_hidden))
            w = kept + term
        return d_hidden, w

    def no_halving(hidden, v, alpha, beta, w):
        return token_call(hidden, v, alpha, beta), w[:, :w.shape[1] // devices]

    w = weigh_call(hidden, alpha, mark)
    d_hidden, w = lax.cond(
        lax.axis_index("rep") < replicas, halve, no_halving, hidden, v, alpha, beta, w
    )

    grad_gain, grad_head, new_global, new_momentum, merged = update_call(
        received, w, gain_wide, head_wide, global_prev, momentum, local
    )
    return d_hidden, grad_gain, grad_head, new_global, new_momentum, merged[None]


def solution(mesh):
    placed = (
        P(("rep", "fsdp"), None),
        P(("rep", "fsdp"), None),
        P(("rep", "fsdp"), None),
        P("fsdp"),
        P("fsdp"),
        P("rep", "fsdp", None),
        P("fsdp", None),
        P("fsdp", None),
    )
    return jax.shard_map(
        body,
        mesh=mesh,
        in_specs=placed,
        out_specs=(
            P(("rep", "fsdp"), None),
            P("rep", "fsdp"),
            P("rep", "fsdp"),
            P("fsdp", None),
            P("fsdp", None),
            P("rep", "fsdp", None),
        ),
        check_vma=False,
    )
```

```python
import jax
import jax.numpy as jnp
from jax import lax
from jax.experimental import pallas as pl
from jax.experimental.pallas import tpu as pltpu
from jax.sharding import PartitionSpec as P

LIST_LEN = 256
CAND = 8
LANES = 128
ROWS = 32

SOFTCAP = 30.0
TEMPER = 2.0
LOSS_SCALE = 512.0
OUTER_RATE = 0.7
MOMENTUM = 0.9
MIXING = 0.5
EPSILON = 1e-06

PLANES = 2
PLANE = 16
TALL, BROAD = 8, 2304
LARGEST = 10.0
STEPS = 32767.0
SHARES = 4
WHOLE_VMEM = 60 * 1024 * 1024
BANDS = 4
VMEM_LIMIT = 16 * 1024 * 1024
SCORE_LIMIT = 16 * 1024 * 1024
TOKEN_LIMIT = 16 * 1024 * 1024
CHUNKS = 4


def chunk_copies(source, kept, sem):
    rows = kept.shape[0] // CHUNKS
    parts = [pl.ds(n * rows, rows) for n in range(CHUNKS)]
    return [pltpu.make_async_copy(source.at[parts[n]], kept.at[parts[n]], sem.at[n]) for n in range(CHUNKS)]


def score_kernel(lengths_ref, ranks_ref, hidden_ref, v_ref, alpha_ref, beta_ref, w_ref, square_ref, dot_ref):
    tokens, width = hidden_ref.shape

    def first(step, carry):
        rows = pl.ds(pl.multiple_of(step * ROWS, ROWS), ROWS)
        square = jnp.zeros((ROWS, LANES), jnp.float32)
        dot = jnp.zeros((ROWS, LANES), jnp.float32)
        for j in range(width // LANES):
            part = slice(j * LANES, (j + 1) * LANES)
            values = hidden_ref[rows, part].astype(jnp.float32)
            square += values * values
            dot += values * v_ref[:, part]
        square_ref[rows, :] = jnp.sum(square, axis=1, keepdims=True)
        dot_ref[rows, :] = jnp.sum(dot, axis=1, keepdims=True)
        return carry

    lax.fori_loop(0, tokens // ROWS, first, 0)

    inverse = lax.rsqrt(square_ref[...] / width + EPSILON)
    dots = dot_ref[...]

    lane = lax.broadcasted_iota(jnp.int32, (1, LANES), 1)
    starts = jnp.zeros((1, LANES), jnp.int32)
    ends = jnp.zeros((1, LANES), jnp.int32)
    ranks = jnp.zeros((1, LANES), jnp.int32)
    end = jnp.int32(0)
    for c in range(CAND):
        start, end = end, end + lengths_ref[0, c]
        starts = jnp.where(lane == c, start, starts)
        ends = jnp.where(lane == c, end, ends)
        ranks = jnp.where(lane == c, ranks_ref[0, c], ranks)
    real = lane < CAND
    root = jnp.sqrt(jnp.where(real, ends - starts, 1).astype(jnp.float32))
    position = lax.broadcasted_iota(jnp.int32, (tokens, LANES), 0)
    member = (position >= starts) & (position < ends)

    raw = jnp.sum(jnp.where(member, inverse * dots, 0.0), axis=0, keepdims=True) / root
    capped = SOFTCAP * jnp.tanh(raw / SOFTCAP)
    weights = jnp.where(real, jnp.exp(capped), 0.0)
    probs = weights / jnp.sum(weights, axis=1, keepdims=True)
    teacher = jnp.where(real, jnp.exp(-ranks.astype(jnp.float32) / TEMPER), 0.0)
    target = teacher / jnp.sum(teacher, axis=1, keepdims=True)
    slope = LOSS_SCALE * (probs - target) * (1.0 - (capped / SOFTCAP) ** 2)
    scale = jnp.sum(jnp.where(member, slope / root, 0.0), axis=1, keepdims=True)

    alpha = inverse * scale
    alpha_ref[...] = jnp.broadcast_to(alpha, alpha_ref.shape)
    beta_ref[...] = jnp.broadcast_to(alpha * inverse * inverse * dots / width, beta_ref.shape)

    for j in range(width // LANES):
        part = slice(j * LANES, (j + 1) * LANES)
        total = jnp.zeros((ROWS, LANES), jnp.float32)
        for row in range(0, tokens, ROWS):
            rows = slice(row, row + ROWS)
            total += alpha_ref[rows, :] * hidden_ref[rows, part].astype(jnp.float32)
        w_ref[:, part] = jnp.sum(total, axis=0, keepdims=True) * (1.0 / LOSS_SCALE)


def score_call(lengths, ranks, hidden, v):
    tokens, width = hidden.shape
    smem = pl.BlockSpec(memory_space=pltpu.SMEM)
    vmem = pl.BlockSpec(memory_space=pltpu.VMEM)
    wide = jax.ShapeDtypeStruct((tokens, LANES), jnp.float32)
    return pl.pallas_call(
        score_kernel,
        out_shape=(wide, wide, jax.ShapeDtypeStruct((1, width), jnp.float32)),
        in_specs=[smem, smem, vmem, vmem],
        out_specs=(vmem, vmem, vmem),
        scratch_shapes=[pltpu.VMEM((tokens, 1), jnp.float32)] * 2,
        compiler_params=pltpu.CompilerParams(vmem_limit_bytes=SCORE_LIMIT),
        cost_estimate=pl.CostEstimate(flops=6 * tokens * width, bytes_accessed=2 * tokens * width, transcendentals=0),
        name="score",
    )(lengths, ranks, hidden, v)


def token_kernel(hidden_hbm_ref, v_ref, alpha_ref, beta_ref, out_ref, hidden_ref, kept_ref, in_sem, out_sem):
    tokens, width = hidden_hbm_ref.shape
    arrivals = chunk_copies(hidden_hbm_ref, hidden_ref, in_sem)
    for arrival in arrivals:
        arrival.start()
    departures = []
    rows_each = tokens // CHUNKS
    for n, arrival in enumerate(arrivals):
        arrival.wait()
        for j in range(width // LANES):
            part = slice(j * LANES, (j + 1) * LANES)
            v = v_ref[:, part]
            for row in range(n * rows_each, (n + 1) * rows_each, ROWS):
                rows = slice(row, row + ROWS)
                values = hidden_ref[rows, part].astype(jnp.float32)
                kept_ref[rows, part] = (alpha_ref[rows, :] * v - beta_ref[rows, :] * values).astype(kept_ref.dtype)
        here = pl.ds(n * rows_each, rows_each)
        departures.append(pltpu.make_async_copy(kept_ref.at[here], out_ref.at[here], out_sem.at[n]))
        departures[-1].start()
    for departure in departures:
        departure.wait()


def token_call(hidden, v, alpha, beta):
    tokens, width = hidden.shape
    vmem = pl.BlockSpec(memory_space=pltpu.VMEM)
    whole = pl.BlockSpec(memory_space=pl.ANY)
    return pl.pallas_call(
        token_kernel,
        out_shape=jax.ShapeDtypeStruct((tokens, width), jnp.bfloat16),
        in_specs=[whole] + [vmem] * 3,
        out_specs=whole,
        scratch_shapes=[pltpu.VMEM((tokens, width), jnp.bfloat16)] * 2 + [pltpu.SemaphoreType.DMA((CHUNKS,))] * 2,
        compiler_params=pltpu.CompilerParams(vmem_limit_bytes=TOKEN_LIMIT),
        cost_estimate=pl.CostEstimate(flops=6 * tokens * width, bytes_accessed=4 * tokens * width, transcendentals=0),
        name="token_grad",
    )(hidden, v, alpha, beta)


def along(array, k):
    devices = lax.axis_size("fsdp")
    return lax.ppermute(array, "fsdp", [(i, i ^ k) for i in range(devices)])


def own_kernel(at_ref, global_ref, out_ref, sem):
    rows = pl.ds(pl.multiple_of(at_ref[0, 0] * TALL, TALL), TALL)
    columns = pl.ds(pl.multiple_of(at_ref[0, 1] * BROAD, BROAD), BROAD)
    copy = pltpu.make_async_copy(global_ref.at[rows, columns], out_ref, sem)
    copy.start()
    copy.wait()


def own_call(at, global_prev):
    return pl.pallas_call(
        own_kernel,
        out_shape=jax.ShapeDtypeStruct((TALL, BROAD), global_prev.dtype),
        in_specs=[pl.BlockSpec(memory_space=pltpu.SMEM), pl.BlockSpec(memory_space=pl.ANY)],
        out_specs=pl.BlockSpec(memory_space=pltpu.VMEM),
        scratch_shapes=[pltpu.SemaphoreType.DMA],
        compiler_params=pltpu.CompilerParams(vmem_limit_bytes=WHOLE_VMEM),
        cost_estimate=pl.CostEstimate(flops=0, bytes_accessed=8 * TALL * BROAD, transcendentals=0),
        name="own",
    )(at, global_prev)


def average_kernel(near_ref, far_ref, global_ref, out_ref, coded_ref, sem):
    average = global_ref[...] - (near_ref[...] + far_ref[...]) * (1.0 / (PLANES * PLANE))
    top = jnp.max(jnp.abs(average), axis=1, keepdims=True)
    unit = jnp.clip(jnp.ceil(top * (STEPS / LARGEST)), 1.0, STEPS)
    steps = jnp.clip(jnp.floor(average * ((STEPS * STEPS / LARGEST) / unit) + 0.5), -STEPS, STEPS)
    copies = []
    for part in range(SHARES):
        coded_ref[part, :, :BROAD] = steps.astype(jnp.int32).astype(coded_ref.dtype)
        coded_ref[part, :, BROAD:] = jnp.broadcast_to(unit, (TALL, LANES)).astype(jnp.int32).astype(coded_ref.dtype)
    for part in range(PLANE // SHARES):
        copies.append(pltpu.make_async_copy(coded_ref, out_ref.at[pl.ds(part * SHARES, SHARES)], sem.at[part]))
    for copy in copies:
        copy.start()
    for copy in copies:
        copy.wait()


def average_call(near, far, own_global):
    vmem = pl.BlockSpec(memory_space=pltpu.VMEM)
    return pl.pallas_call(
        average_kernel,
        out_shape=jax.ShapeDtypeStruct((PLANE, TALL, BROAD + LANES), jnp.int16),
        in_specs=[vmem, vmem, vmem],
        out_specs=pl.BlockSpec(memory_space=pl.ANY),
        scratch_shapes=[pltpu.VMEM((SHARES, TALL, BROAD + LANES), jnp.int16), pltpu.SemaphoreType.DMA((PLANE // SHARES,))],
        compiler_params=pltpu.CompilerParams(vmem_limit_bytes=VMEM_LIMIT),
        cost_estimate=pl.CostEstimate(flops=10 * near.size, bytes_accessed=40 * near.size, transcendentals=0),
        name="average",
    )(near, far, own_global)


def update_kernel(coded_ref, w_ref, gain_ref, head_ref, global_ref, momentum_ref, local_ref,
                  grad_gain_ref, grad_head_ref, *refs):
    outs, kept, sem = refs[:3], refs[3:6], refs[6]
    rows, width = global_ref.shape
    across = width // BROAD
    new_global_ref, new_momentum_ref, merged_ref = kept
    copies = []
    band_rows, band_pieces = rows // BANDS, PLANE // BANDS
    for band in range(BANDS):
        for p in range(band * band_pieces, (band + 1) * band_pieces):
            row = slice(p // across * TALL, (p // across + 1) * TALL)
            scale = coded_ref[p, :, BROAD:].astype(jnp.int32).astype(jnp.float32) * (LARGEST / (STEPS * STEPS))
            for j in range(BROAD // LANES):
                at = p % across * BROAD + j * LANES
                part = slice(at, at + LANES)
                steps = coded_ref[p, :, j * LANES:(j + 1) * LANES].astype(jnp.int32).astype(jnp.float32)
                average = steps * scale
                new_momentum = MOMENTUM * momentum_ref[row, part] + average
                new_global = global_ref[row, part] - OUTER_RATE * (MOMENTUM * new_momentum + average)
                new_momentum_ref[row, part] = new_momentum
                new_global_ref[row, part] = new_global
        row = slice(band * band_rows, (band + 1) * band_rows)
        for j in range(width // LANES):
            part = slice(j * LANES, (j + 1) * LANES)
            merged = MIXING * local_ref[row, part].astype(jnp.float32) + (1.0 - MIXING) * new_global_ref[row, part]
            merged_ref[row, part] = merged.astype(merged_ref.dtype)
        for n in range(3):
            copies.append(pltpu.make_async_copy(kept[n].at[row, :], outs[n].at[row, :], sem.at[n, band]))
            copies[-1].start()
    w = w_ref[...]
    grad_gain_ref[...] = w * head_ref[...]
    grad_head_ref[...] = w * gain_ref[...]
    for copy in copies:
        copy.wait()


def update_call(coded, w, gain, head, global_prev, momentum, local):
    rows, width = global_prev.shape
    vmem = pl.BlockSpec(memory_space=pltpu.VMEM)
    whole = pl.BlockSpec(memory_space=pl.ANY)
    wide, narrow = jnp.float32, jnp.bfloat16
    grad = jax.ShapeDtypeStruct(w.shape, wide)
    return pl.pallas_call(
        update_kernel,
        out_shape=(grad, grad) + tuple(jax.ShapeDtypeStruct((rows, width), t) for t in (wide, wide, narrow)),
        in_specs=[vmem] * 7,
        out_specs=(vmem,) * 2 + (whole,) * 3,
        scratch_shapes=[pltpu.VMEM((rows, width), t) for t in (wide, wide, narrow)]
        + [pltpu.SemaphoreType.DMA((3, BANDS))],
        compiler_params=pltpu.CompilerParams(vmem_limit_bytes=VMEM_LIMIT),
        cost_estimate=pl.CostEstimate(flops=10 * rows * width, bytes_accessed=22 * rows * width, transcendentals=0),
        name="update",
    )(coded, w, gain, head, global_prev, momentum, local)


def body(hidden, lengths, ranks, gain, head, local_frag, global_prev, momentum):
    barrier = lax.optimization_barrier
    replicas, devices = lax.axis_size("rep"), lax.axis_size("fsdp")
    planes = [[PLANE * z + i for i in range(PLANE)] for z in range(PLANES)]
    here = lax.axis_index("fsdp")
    local = local_frag[0]

    pieces = local.reshape(8, TALL, 2, BROAD).transpose(0, 2, 1, 3).reshape(PLANE, TALL, BROAD)
    pieces, gain, head = barrier((pieces, gain, head))
    gain_wide, head_wide = gain.astype(jnp.float32)[None], head.astype(jnp.float32)[None]
    mine = lax.all_to_all(pieces, "rep", 0, 0, tiled=True, axis_index_groups=planes)

    v = gain_wide * head_wide
    for bit in (1, 2, 4):
        other = along(v, bit)
        v = jnp.where(here & bit == 0, jnp.concatenate([v, other], 1), jnp.concatenate([other, v], 1))
    owned = lax.rem(lax.axis_index("rep"), PLANE)
    across = global_prev.shape[1] // BROAD
    own_global = own_call(jnp.stack([owned // across, owned % across]).astype(jnp.int32)[None], global_prev)

    mine, own_global = barrier((mine, own_global))
    near = jnp.sum(mine.astype(jnp.float32), axis=0)
    far = lax.ppermute(near, "rep", [(i, (i + PLANE) % replicas) for i in range(replicas)])

    alpha, beta, w = score_call(lengths, ranks, hidden, v)
    far, alpha, beta, w = barrier((far, alpha, beta, w))

    coded = average_call(near, far, own_global)
    coded, w = barrier((coded, w))
    received = lax.all_to_all(coded, "rep", 0, 0, tiled=True, axis_index_groups=planes)

    def halve(hidden, v, alpha, beta, w):
        d_hidden = None
        for bit in (4, 2, 1):
            half = w.shape[1] // 2
            low, high = w[:, :half], w[:, half:]
            kept, sent = jnp.where(here & bit == 0, low, high), jnp.where(here & bit == 0, high, low)
            term = along(sent, bit)
            if bit == 4:
                d_hidden = token_call(hidden, v, alpha, beta)
                term, d_hidden = barrier((term, d_hidden))
            w = kept + term
        return d_hidden, w

    def no_halving(hidden, v, alpha, beta, w):
        return token_call(hidden, v, alpha, beta), w[:, :w.shape[1] // devices]

    d_hidden, w = lax.cond(
        lax.axis_index("rep") < replicas, halve, no_halving, hidden, v, alpha, beta, w
    )

    grad_gain, grad_head, new_global, new_momentum, merged = update_call(
        received, w, gain_wide, head_wide, global_prev, momentum, local
    )
    return d_hidden, grad_gain, grad_head, new_global, new_momentum, merged[None]


def solution(mesh):
    placed = (
        P(("rep", "fsdp"), None),
        P(("rep", "fsdp"), None),
        P(("rep", "fsdp"), None),
        P("fsdp"),
        P("fsdp"),
        P("rep", "fsdp", None),
        P("fsdp", None),
        P("fsdp", None),
    )
    return jax.shard_map(
        body,
        mesh=mesh,
        in_specs=placed,
        out_specs=(
            P(("rep", "fsdp"), None),
            P("rep", "fsdp"),
            P("rep", "fsdp"),
            P("fsdp", None),
            P("fsdp", None),
            P("rep", "fsdp", None),
        ),
        check_vma=False,
    )
```

```python
import jax
import jax.numpy as jnp
from jax import lax
from jax.experimental import pallas as pl
from jax.experimental.pallas import tpu as pltpu
from jax.sharding import PartitionSpec as P

LIST_LEN = 256
CAND = 8
LANES = 128
ROWS = 32

SOFTCAP = 30.0
TEMPER = 2.0
LOSS_SCALE = 512.0
OUTER_RATE = 0.7
MOMENTUM = 0.9
MIXING = 0.5
EPSILON = 1e-06

PLANES = 2
PLANE = 16
TALL, BROAD = 8, 2304
LARGEST = 10.0
STEPS = 32767.0
SHARES = 4
WHOLE_VMEM = 60 * 1024 * 1024
BANDS = 4
VMEM_LIMIT = 16 * 1024 * 1024
SCORE_LIMIT = 16 * 1024 * 1024
TOKEN_LIMIT = 16 * 1024 * 1024
CHUNKS = 4


def chunk_copies(source, kept, sem):
    rows = kept.shape[0] // CHUNKS
    parts = [pl.ds(n * rows, rows) for n in range(CHUNKS)]
    return [pltpu.make_async_copy(source.at[parts[n]], kept.at[parts[n]], sem.at[n]) for n in range(CHUNKS)]


def score_kernel(lengths_ref, ranks_ref, hidden_ref, v_ref, alpha_ref, beta_ref, w_ref, square_ref, dot_ref):
    tokens, width = hidden_ref.shape

    def first(step, carry):
        rows = pl.ds(pl.multiple_of(step * ROWS, ROWS), ROWS)
        square = jnp.zeros((ROWS, LANES), jnp.float32)
        dot = jnp.zeros((ROWS, LANES), jnp.float32)
        for j in range(width // LANES):
            part = slice(j * LANES, (j + 1) * LANES)
            values = hidden_ref[rows, part].astype(jnp.float32)
            square += values * values
            dot += values * v_ref[:, part]
        square_ref[rows, :] = jnp.sum(square, axis=1, keepdims=True)
        dot_ref[rows, :] = jnp.sum(dot, axis=1, keepdims=True)
        return carry

    lax.fori_loop(0, tokens // ROWS, first, 0)

    inverse = lax.rsqrt(square_ref[...] / width + EPSILON)
    dots = dot_ref[...]

    lane = lax.broadcasted_iota(jnp.int32, (1, LANES), 1)
    starts = jnp.zeros((1, LANES), jnp.int32)
    ends = jnp.zeros((1, LANES), jnp.int32)
    ranks = jnp.zeros((1, LANES), jnp.int32)
    end = jnp.int32(0)
    for c in range(CAND):
        start, end = end, end + lengths_ref[0, c]
        starts = jnp.where(lane == c, start, starts)
        ends = jnp.where(lane == c, end, ends)
        ranks = jnp.where(lane == c, ranks_ref[0, c], ranks)
    real = lane < CAND
    root = jnp.sqrt(jnp.where(real, ends - starts, 1).astype(jnp.float32))
    position = lax.broadcasted_iota(jnp.int32, (tokens, LANES), 0)
    member = (position >= starts) & (position < ends)

    raw = jnp.sum(jnp.where(member, inverse * dots, 0.0), axis=0, keepdims=True) / root
    capped = SOFTCAP * jnp.tanh(raw / SOFTCAP)
    weights = jnp.where(real, jnp.exp(capped), 0.0)
    probs = weights / jnp.sum(weights, axis=1, keepdims=True)
    teacher = jnp.where(real, jnp.exp(-ranks.astype(jnp.float32) / TEMPER), 0.0)
    target = teacher / jnp.sum(teacher, axis=1, keepdims=True)
    slope = LOSS_SCALE * (probs - target) * (1.0 - (capped / SOFTCAP) ** 2)
    scale = jnp.sum(jnp.where(member, slope / root, 0.0), axis=1, keepdims=True)

    alpha = inverse * scale
    alpha_ref[...] = jnp.broadcast_to(alpha, alpha_ref.shape)
    beta_ref[...] = jnp.broadcast_to(alpha * inverse * inverse * dots / width, beta_ref.shape)

    for j in range(width // LANES):
        part = slice(j * LANES, (j + 1) * LANES)
        total = jnp.zeros((ROWS, LANES), jnp.float32)
        for row in range(0, tokens, ROWS):
            rows = slice(row, row + ROWS)
            total += alpha_ref[rows, :] * hidden_ref[rows, part].astype(jnp.float32)
        w_ref[:, part] = jnp.sum(total, axis=0, keepdims=True) * (1.0 / LOSS_SCALE)


def score_call(lengths, ranks, hidden, v):
    tokens, width = hidden.shape
    smem = pl.BlockSpec(memory_space=pltpu.SMEM)
    vmem = pl.BlockSpec(memory_space=pltpu.VMEM)
    wide = jax.ShapeDtypeStruct((tokens, LANES), jnp.float32)
    return pl.pallas_call(
        score_kernel,
        out_shape=(wide, wide, jax.ShapeDtypeStruct((1, width), jnp.float32)),
        in_specs=[smem, smem, vmem, vmem],
        out_specs=(vmem, vmem, vmem),
        scratch_shapes=[pltpu.VMEM((tokens, 1), jnp.float32)] * 2,
        compiler_params=pltpu.CompilerParams(vmem_limit_bytes=SCORE_LIMIT),
        cost_estimate=pl.CostEstimate(flops=6 * tokens * width, bytes_accessed=2 * tokens * width, transcendentals=0),
        name="score",
    )(lengths, ranks, hidden, v)


def token_kernel(hidden_hbm_ref, v_ref, alpha_ref, beta_ref, out_ref, hidden_ref, kept_ref, in_sem, out_sem):
    tokens, width = hidden_hbm_ref.shape
    arrivals = chunk_copies(hidden_hbm_ref, hidden_ref, in_sem)
    for arrival in arrivals:
        arrival.start()
    departures = []
    rows_each = tokens // CHUNKS
    for n, arrival in enumerate(arrivals):
        arrival.wait()
        for j in range(width // LANES):
            part = slice(j * LANES, (j + 1) * LANES)
            v = v_ref[:, part]
            for row in range(n * rows_each, (n + 1) * rows_each, ROWS):
                rows = slice(row, row + ROWS)
                values = hidden_ref[rows, part].astype(jnp.float32)
                kept_ref[rows, part] = (alpha_ref[rows, :] * v - beta_ref[rows, :] * values).astype(kept_ref.dtype)
        here = pl.ds(n * rows_each, rows_each)
        departures.append(pltpu.make_async_copy(kept_ref.at[here], out_ref.at[here], out_sem.at[n]))
        departures[-1].start()
    for departure in departures:
        departure.wait()


def token_call(hidden, v, alpha, beta):
    tokens, width = hidden.shape
    vmem = pl.BlockSpec(memory_space=pltpu.VMEM)
    whole = pl.BlockSpec(memory_space=pl.ANY)
    return pl.pallas_call(
        token_kernel,
        out_shape=jax.ShapeDtypeStruct((tokens, width), jnp.bfloat16),
        in_specs=[whole] + [vmem] * 3,
        out_specs=whole,
        scratch_shapes=[pltpu.VMEM((tokens, width), jnp.bfloat16)] * 2 + [pltpu.SemaphoreType.DMA((CHUNKS,))] * 2,
        compiler_params=pltpu.CompilerParams(vmem_limit_bytes=TOKEN_LIMIT),
        cost_estimate=pl.CostEstimate(flops=6 * tokens * width, bytes_accessed=4 * tokens * width, transcendentals=0),
        name="token_grad",
    )(hidden, v, alpha, beta)


def along(array, k):
    devices = lax.axis_size("fsdp")
    return lax.ppermute(array, "fsdp", [(i, i ^ k) for i in range(devices)])


def own_kernel(at_ref, global_ref, out_ref, sem):
    rows = pl.ds(pl.multiple_of(at_ref[0, 0] * TALL, TALL), TALL)
    columns = pl.ds(pl.multiple_of(at_ref[0, 1] * BROAD, BROAD), BROAD)
    copy = pltpu.make_async_copy(global_ref.at[rows, columns], out_ref, sem)
    copy.start()
    copy.wait()


def own_call(at, global_prev):
    return pl.pallas_call(
        own_kernel,
        out_shape=jax.ShapeDtypeStruct((TALL, BROAD), global_prev.dtype),
        in_specs=[pl.BlockSpec(memory_space=pltpu.SMEM), pl.BlockSpec(memory_space=pl.ANY)],
        out_specs=pl.BlockSpec(memory_space=pltpu.VMEM),
        scratch_shapes=[pltpu.SemaphoreType.DMA],
        compiler_params=pltpu.CompilerParams(vmem_limit_bytes=WHOLE_VMEM),
        cost_estimate=pl.CostEstimate(flops=0, bytes_accessed=8 * TALL * BROAD, transcendentals=0),
        name="own",
    )(at, global_prev)


def average_kernel(near_ref, far_ref, global_ref, out_ref, coded_ref, sem):
    average = global_ref[...] - (near_ref[...] + far_ref[...]) * (1.0 / (PLANES * PLANE))
    top = jnp.max(jnp.abs(average), axis=1, keepdims=True)
    unit = jnp.clip(jnp.ceil(top * (STEPS / LARGEST)), 1.0, STEPS)
    steps = jnp.clip(jnp.floor(average * ((STEPS * STEPS / LARGEST) / unit) + 0.5), -STEPS, STEPS)
    copies = []
    for part in range(SHARES):
        coded_ref[part, :, :BROAD] = steps.astype(jnp.int32).astype(coded_ref.dtype)
        coded_ref[part, :, BROAD:] = jnp.broadcast_to(unit, (TALL, LANES)).astype(jnp.int32).astype(coded_ref.dtype)
    for part in range(PLANE // SHARES):
        copies.append(pltpu.make_async_copy(coded_ref, out_ref.at[pl.ds(part * SHARES, SHARES)], sem.at[part]))
    for copy in copies:
        copy.start()
    for copy in copies:
        copy.wait()


def average_call(near, far, own_global):
    vmem = pl.BlockSpec(memory_space=pltpu.VMEM)
    return pl.pallas_call(
        average_kernel,
        out_shape=jax.ShapeDtypeStruct((PLANE, TALL, BROAD + LANES), jnp.int16),
        in_specs=[vmem, vmem, vmem],
        out_specs=pl.BlockSpec(memory_space=pl.ANY),
        scratch_shapes=[pltpu.VMEM((SHARES, TALL, BROAD + LANES), jnp.int16), pltpu.SemaphoreType.DMA((PLANE // SHARES,))],
        compiler_params=pltpu.CompilerParams(vmem_limit_bytes=VMEM_LIMIT),
        cost_estimate=pl.CostEstimate(flops=10 * near.size, bytes_accessed=40 * near.size, transcendentals=0),
        name="average",
    )(near, far, own_global)


def update_kernel(coded_ref, w_ref, gain_ref, head_ref, global_ref, scaled_hbm_ref, local_ref,
                  grad_gain_ref, grad_head_ref, *refs):
    outs, kept, sem, grads, grad_sem, scaled_ref, in_sem = refs[:3], refs[3:6], *refs[6:11]
    rows, width = global_ref.shape
    across = width // BROAD
    new_global_ref, new_momentum_ref, merged_ref = kept
    band_rows, band_pieces = rows // BANDS, PLANE // BANDS
    arrivals = []
    for band in range(BANDS):
        part = pl.ds(band * band_rows, band_rows)
        arrivals.append(pltpu.make_async_copy(scaled_hbm_ref.at[part], scaled_ref.at[part], in_sem.at[band]))
        arrivals[-1].start()
    grads[0] = w_ref[...] * head_ref[...]
    grads[1] = w_ref[...] * gain_ref[...]
    copies = [pltpu.make_async_copy(grads.at[n], out, grad_sem.at[n]) for n, out in enumerate((grad_gain_ref, grad_head_ref))]
    for copy in copies:
        copy.start()
    for band in range(BANDS):
        arrivals[band].wait()
        for p in range(band * band_pieces, (band + 1) * band_pieces):
            row = slice(p // across * TALL, (p // across + 1) * TALL)
            scale = coded_ref[p, :, BROAD:].astype(jnp.int32).astype(jnp.float32) * (LARGEST / (STEPS * STEPS))
            for j in range(BROAD // LANES):
                at = p % across * BROAD + j * LANES
                part = slice(at, at + LANES)
                steps = coded_ref[p, :, j * LANES:(j + 1) * LANES].astype(jnp.int32).astype(jnp.float32)
                average = steps * scale
                new_momentum = scaled_ref[row, part] + average
                new_global = global_ref[row, part] - OUTER_RATE * (MOMENTUM * new_momentum + average)
                new_momentum_ref[row, part] = new_momentum
                new_global_ref[row, part] = new_global
        row = slice(band * band_rows, (band + 1) * band_rows)
        for j in range(width // LANES):
            part = slice(j * LANES, (j + 1) * LANES)
            merged = MIXING * local_ref[row, part].astype(jnp.float32) + (1.0 - MIXING) * new_global_ref[row, part]
            merged_ref[row, part] = merged.astype(merged_ref.dtype)
        for n in range(3):
            copies.append(pltpu.make_async_copy(kept[n].at[row, :], outs[n].at[row, :], sem.at[n, band]))
            copies[-1].start()
    for copy in copies:
        copy.wait()


def update_call(coded, w, gain, head, global_prev, scaled, local):
    rows, width = global_prev.shape
    vmem = pl.BlockSpec(memory_space=pltpu.VMEM)
    whole = pl.BlockSpec(memory_space=pl.ANY)
    wide, narrow = jnp.float32, jnp.bfloat16
    grad = jax.ShapeDtypeStruct(w.shape, wide)
    return pl.pallas_call(
        update_kernel,
        out_shape=(grad, grad) + tuple(jax.ShapeDtypeStruct((rows, width), t) for t in (wide, wide, narrow)),
        in_specs=[vmem] * 5 + [whole, vmem],
        out_specs=(whole,) * 5,
        scratch_shapes=[pltpu.VMEM((rows, width), t) for t in (wide, wide, narrow)]
        + [pltpu.SemaphoreType.DMA((3, BANDS)), pltpu.VMEM((2, *w.shape), wide), pltpu.SemaphoreType.DMA((2,))]
        + [pltpu.VMEM((rows, width), wide), pltpu.SemaphoreType.DMA((BANDS,))],
        compiler_params=pltpu.CompilerParams(vmem_limit_bytes=VMEM_LIMIT),
        cost_estimate=pl.CostEstimate(flops=10 * rows * width, bytes_accessed=22 * rows * width, transcendentals=0),
        name="update",
    )(coded, w, gain, head, global_prev, scaled, local)


def body(hidden, lengths, ranks, gain, head, local_frag, global_prev, momentum):
    barrier = lax.optimization_barrier
    replicas, devices = lax.axis_size("rep"), lax.axis_size("fsdp")
    planes = [[PLANE * z + i for i in range(PLANE)] for z in range(PLANES)]
    here = lax.axis_index("fsdp")
    local = local_frag[0]

    pieces = local.reshape(8, TALL, 2, BROAD).transpose(0, 2, 1, 3).reshape(PLANE, TALL, BROAD)
    pieces, gain, head = barrier((pieces, gain, head))
    gain_wide, head_wide = gain.astype(jnp.float32)[None], head.astype(jnp.float32)[None]
    mine = lax.all_to_all(pieces, "rep", 0, 0, tiled=True, axis_index_groups=planes)

    v = gain_wide * head_wide
    for bit in (1, 2, 4):
        other = along(v, bit)
        v = jnp.where(here & bit == 0, jnp.concatenate([v, other], 1), jnp.concatenate([other, v], 1))
    owned = lax.rem(lax.axis_index("rep"), PLANE)
    across = global_prev.shape[1] // BROAD
    own_global = own_call(jnp.stack([owned // across, owned % across]).astype(jnp.int32)[None], global_prev)

    mine, own_global = barrier((mine, own_global))
    near = jnp.sum(mine.astype(jnp.float32), axis=0)
    far = lax.ppermute(near, "rep", [(i, (i + PLANE) % replicas) for i in range(replicas)])

    alpha, beta, w = score_call(lengths, ranks, hidden, v)
    far, alpha, beta, w = barrier((far, alpha, beta, w))

    coded = average_call(near, far, own_global)
    coded, w = barrier((coded, w))
    received = lax.all_to_all(coded, "rep", 0, 0, tiled=True, axis_index_groups=planes)

    def halve(hidden, v, alpha, beta, momentum, w):
        d_hidden = token_call(hidden, v, alpha, beta)
        scaled = MOMENTUM * momentum
        for bit in (4, 2, 1):
            half = w.shape[1] // 2
            low, high = w[:, :half], w[:, half:]
            kept, sent = jnp.where(here & bit == 0, low, high), jnp.where(here & bit == 0, high, low)
            term = along(sent, bit)
            if bit == 4:
                term, d_hidden, momentum = barrier((term, d_hidden, momentum))
                scaled = MOMENTUM * momentum
            if bit == 2:
                term, scaled = barrier((term, scaled))
            w = kept + term
        return d_hidden, scaled, w

    def no_halving(hidden, v, alpha, beta, momentum, w):
        return token_call(hidden, v, alpha, beta), MOMENTUM * momentum, w[:, :w.shape[1] // devices]

    d_hidden, scaled, w = lax.cond(
        lax.axis_index("rep") < replicas, halve, no_halving, hidden, v, alpha, beta, momentum, w
    )

    grad_gain, grad_head, new_global, new_momentum, merged = update_call(
        received, w, gain_wide, head_wide, global_prev, scaled, local
    )
    return d_hidden, grad_gain, grad_head, new_global, new_momentum, merged[None]


def solution(mesh):
    placed = (
        P(("rep", "fsdp"), None),
        P(("rep", "fsdp"), None),
        P(("rep", "fsdp"), None),
        P("fsdp"),
        P("fsdp"),
        P("rep", "fsdp", None),
        P("fsdp", None),
        P("fsdp", None),
    )
    return jax.shard_map(
        body,
        mesh=mesh,
        in_specs=placed,
        out_specs=(
            P(("rep", "fsdp"), None),
            P("rep", "fsdp"),
            P("rep", "fsdp"),
            P("fsdp", None),
            P("fsdp", None),
            P("rep", "fsdp", None),
        ),
        check_vma=False,
    )
```
